32 devices in a mesh: aux: 16 (over z, y, x), orb: 2 (over core).
Axes of the slice: x: 2, y: 2, z: 4, core: 2. Of those that a mesh axis runs over, the one named last changes fastest.
Arguments:
- integrals: bfloat16 [384, 8, 4096], P('aux', 'orb'), may hold values from -6 to 6
- coefficients: bfloat16 [6144, 192], P('orb'), may hold values from -0.375 to 0.375
- metric: bfloat16 [384, 384], P('aux'), may hold values from -0.3125 to 0.3125
- mu_blocks: int32 [16, 8], P('aux', 'orb'), may hold values from 0 to 95
- nu_blocks: int32 [16, 8], P('aux', 'orb'), may hold values from 0 to 47
- counts: int32 [16, 2], P('aux', 'orb'), may hold values from 1 to 4, as said below
Outputs:
- pair_major: bfloat16 [192, 6144, 384], P('aux', 'orb')
The draws below stay inside these ranges and needn't reach their ends.
Inputs may be any that keep to these rules, and one draw needn't show every extreme that they name: `counts`: each entry is between 1 and 4; in every draw some device holds exactly 4 live slots. `mu_blocks`: block pairs may repeat; repeated pairs add.
All inputs are finite; a program needn't handle non-finite values.
Results may differ from the reference program's by a relative error of at most 0.0049.
Values may be sent and summed in bfloat16 or wider, within the bound.
A program may use at most 192 MiB of HBM per device.

```python
import jax
import jax.numpy as jnp
from jax import lax

BLK = 64
NBF = 6144
OCC = 192
AUX_DEV = 24
K = 4
AUX = 384
NBLK = 96
NU_DEV = 3072
NU_BLK = 48
N_AUX = 16
N_ORB = 2


def draw_counts(key, part):
    key = jax.random.fold_in(key, 3)
    draw_key, spot_key = jax.random.split(key)
    values = jax.random.randint(draw_key, (N_AUX, N_ORB), 1, K + 1)
    chosen = jax.random.randint(spot_key, (), 0, N_AUX * N_ORB)
    flattened = values.reshape(-1)
    flattened = jnp.where(jnp.arange(N_AUX * N_ORB) == chosen, K, flattened)
    return flattened.reshape(N_AUX, N_ORB).astype(jnp.int32)


def set_ends(result, stream_key, least, high):
    longest = result.shape.index(max(result.shape))
    spots = []
    for shift in (0, 1):
        where = [jax.random.randint(jax.random.fold_in(stream_key, axis), (), 0, length) for axis, length in enumerate(result.shape)]
        where[longest] = (where[longest] + shift) % result.shape[longest]
        spots.append(tuple(where))
    return result.at[spots[0]].set(least).at[spots[1]].set(high)


def shard_levels(own_key, extent, cuts, low, largest):
    loudness = 1.0
    for axis_at, shards_of in cuts:
        draws = jax.random.uniform(jax.random.fold_in(jax.random.fold_in(own_key, 6), axis_at), (shards_of,), jnp.float32, low / len(cuts), largest / len(cuts))
        loudness = loudness * jnp.repeat(jnp.exp(draws), extent[axis_at] // shards_of).reshape((-1,) + (1,) * (len(extent) - 1 - axis_at))
    return loudness


def normal_values(own_key, extent, spread, most, pieces=(), dtype=jnp.bfloat16):
    gain = shard_levels(own_key, extent, pieces, -0.22, 0.18) if pieces else 1.0
    array = jax.random.normal(own_key, extent, jnp.float32) * spread * gain
    return jnp.minimum(jnp.maximum(array, -most), most).astype(dtype)


def setup_inputs(seed: int = 0) -> dict:
    key_of = jax.random.split(jax.random.key(seed), 7)
    integrals = normal_values(key_of[0], (AUX, N_ORB * K, BLK * BLK), 1.0, 6.0, ((0, 16), (1, 2)))
    coefficients = normal_values(key_of[1], (NBF, OCC), (BLK * K) ** -0.5, 0.375, ((0, 2),))
    metric = normal_values(key_of[2], (AUX, AUX), AUX ** -0.5, 0.3125, ((0, 16),))
    mu_blocks = set_ends(jax.random.randint(key_of[3], (N_AUX, N_ORB * K), 0, NBLK), jax.random.fold_in(key_of[3], 1), 0, NBLK - 1).astype(jnp.int32)
    nu_blocks = set_ends(jax.random.randint(key_of[4], (N_AUX, N_ORB * K), 0, NU_BLK), jax.random.fold_in(key_of[4], 1), 0, NU_BLK - 1).astype(jnp.int32)
    counts = draw_counts(jax.random.fold_in(key_of[6], 71), 0)
    return dict(integrals=integrals, coefficients=coefficients, metric=metric, mu_blocks=mu_blocks, nu_blocks=nu_blocks, counts=counts)


def half_slab(slab_ints, mu_row, nu_row, count_row, coef_wide):
    partial_value = jnp.zeros((AUX_DEV, OCC, NBF), jnp.float32)

    def add_pair(slot, partial_value):
        owner = slot // K
        int_block = lax.dynamic_index_in_dim(slab_ints, slot, 1, keepdims=False)
        int_block = int_block.reshape(AUX_DEV, BLK, BLK).astype(jnp.float32)
        mu_start = (mu_row[slot] * BLK).astype(jnp.int32)
        coef_rows = lax.dynamic_slice_in_dim(coef_wide, mu_start, BLK, 0)
        product = jnp.einsum("pmn,mi->pin", int_block, coef_rows)
        live_mask = jnp.where(slot % K < count_row[owner], 1.0, 0.0).astype(jnp.float32)
        offset = (owner * NU_DEV + nu_row[slot] * BLK).astype(jnp.int32)
        current = lax.dynamic_slice_in_dim(partial_value, offset, BLK, 2)
        return lax.dynamic_update_slice_in_dim(partial_value, current + live_mask * product, offset, 2)

    partial_value = lax.fori_loop(0, N_ORB * K, add_pair, partial_value)
    return partial_value.astype(jnp.bfloat16)


def reference(integrals, coefficients, metric, mu_blocks, nu_blocks, counts):
    slabs = integrals.reshape(N_AUX, AUX_DEV, N_ORB * K, BLK * BLK)
    coef_wide = coefficients.astype(jnp.float32)

    def one_slab(inputs):
        slab_ints, mu_row, nu_row, count_row = inputs
        return half_slab(slab_ints, mu_row, nu_row, count_row, coef_wide)

    half = lax.map(one_slab, (slabs, mu_blocks, nu_blocks, counts))
    half = half.reshape(AUX, OCC, NBF)

    def one_orbital(column):
        return jnp.dot(column.T, metric.T, preferred_element_type=jnp.float32).astype(jnp.bfloat16)

    return lax.map(one_orbital, jnp.moveaxis(half, 1, 0))
```

```python
import functools

import jax
import jax.numpy as jnp
from jax import lax
from jax.experimental import pallas as pl
from jax.experimental.pallas import tpu as pltpu
from jax.sharding import PartitionSpec as P

BLK = 64
MESH = pl.DeviceIdType.MESH


def exchange_kernel(n, msg_ref, recv_ref, send_sem, recv_sem, own_sem):
    me = lax.axis_index("aux")
    orb = lax.axis_index("orb")
    barrier = pltpu.get_barrier_semaphore()
    for k in range(1, n):
        pl.semaphore_signal(
            barrier, inc=1, device_id=(lax.rem(me + k, n), orb), device_id_type=MESH
        )
    pl.semaphore_wait(barrier, n - 1)
    order = sorted(range(1, n), key=lambda k: abs(k - n // 2))
    copies = []
    for k in order:
        peer = lax.rem(me + k, n)
        copy = pltpu.make_async_remote_copy(
            src_ref=msg_ref.at[peer],
            dst_ref=recv_ref.at[me],
            send_sem=send_sem.at[k],
            recv_sem=recv_sem.at[k],
            device_id=(peer, orb),
            device_id_type=MESH,
        )
        copy.start()
        copies.append((k, copy))
    own = pltpu.make_async_copy(msg_ref.at[me], recv_ref.at[me], own_sem)
    own.start()
    own.wait()
    for k, copy in copies:
        copy.wait_send()
        source = lax.rem(me - k + n, n)
        pltpu.make_async_remote_copy(
            src_ref=msg_ref.at[source],
            dst_ref=recv_ref.at[source],
            send_sem=send_sem.at[k],
            recv_sem=recv_sem.at[k],
            device_id=(source, orb),
            device_id_type=MESH,
        ).wait_recv()


def exchange(msg, n):
    return pl.pallas_call(
        functools.partial(exchange_kernel, n),
        out_shape=jax.ShapeDtypeStruct(msg.shape, msg.dtype),
        in_specs=[pl.BlockSpec(memory_space=pl.ANY)],
        out_specs=pl.BlockSpec(memory_space=pl.ANY),
        scratch_shapes=[
            pltpu.SemaphoreType.DMA((n,)),
            pltpu.SemaphoreType.DMA((n,)),
            pltpu.SemaphoreType.DMA,
        ],
        compiler_params=pltpu.CompilerParams(collective_id=0, has_side_effects=True),
        name="exchange_slots",
    )(msg)


def contract_kernel(
    n_aux, slots, aux_dev, pad, occ_local, nu_blk, levels,
    nu_ref, recv_ref, met_ref, out_ref,
    padded, lhs, wgt, obuf, zero, sems, count, lists,
):
    total = n_aux * slots
    lanes = occ_local * BLK
    aux_total = out_ref.shape[2]

    def clear(b, _):
        count[b] = 0
        return 0

    lax.fori_loop(0, nu_blk, clear, 0)

    def enlist(e, _):
        b = nu_ref[e]

        @pl.when(b >= 0)
        def _():
            c = count[b]
            lists[b * n_aux + c] = e
            count[b] = c + 1

        return 0

    lax.fori_loop(0, total, enlist, 0)

    zero[...] = jnp.zeros_like(zero)
    padded[total] = jnp.zeros((pad, lanes), padded.dtype)

    def spread(a, _):
        rows = recv_ref[a]
        for s in range(slots):
            part = rows[s * aux_dev : (s + 1) * aux_dev]
            padded[a * slots + s] = jnp.concatenate(
                [part, jnp.zeros((pad - aux_dev, lanes), part.dtype)], axis=0
            )
        return 0

    lax.fori_loop(0, n_aux, spread, 0)

    def out_copy(src, b, which):
        return pltpu.make_async_copy(
            src, out_ref.at[:, pl.ds(pl.multiple_of(b * BLK, BLK), BLK), :], sems.at[which]
        )

    nbuf = obuf.shape[0]

    def block(b, _):
        which = lax.rem(b, nbuf)
        c = count[b]

        @pl.when(b >= nbuf)
        def _():
            out_copy(zero, b - nbuf, which).wait()

        @pl.when(c == 0)
        def _():
            out_copy(zero, b, which).start()

        low = 0
        for level in levels:

            @pl.when((c > low) & (c <= level))
            def _(level=level):
                for j in range(level):
                    e = jnp.where(j < c, lists[b * n_aux + jnp.minimum(j, c - 1)], total)
                    a = jnp.where(j < c, e // slots, 0)
                    lhs[j * pad : (j + 1) * pad, :] = padded[e]
                    wgt[j * pad : (j + 1) * pad, :] = met_ref[a]
                depth = level * pad
                step = 128 if lanes % 128 == 0 else lanes
                for at in range(0, lanes, step):
                    res = lax.dot_general(
                        lhs[:depth, at : at + step],
                        wgt[:depth, :],
                        (((0,), (0,)), ((), ())),
                        preferred_element_type=jnp.float32,
                    )
                    obuf[which, at // BLK : (at + step) // BLK] = res.astype(
                        obuf.dtype
                    ).reshape(step // BLK, BLK, aux_total)
                out_copy(obuf.at[which], b, which).start()

            low = level
        return 0

    lax.fori_loop(0, nu_blk, block, 0)
    for b in range(max(0, nu_blk - nbuf), nu_blk):
        out_copy(zero, b, b % nbuf).wait()


def contract(nu_lists, recv, met, occ_local, nu_local):
    n_aux, rows, lanes = recv.shape
    slots = nu_lists.shape[0] // n_aux
    aux_dev = rows // slots
    pad = met.shape[1]
    aux_total = met.shape[2]
    nu_blk = nu_local // BLK
    levels = [v for v in (2, 4, 8, 16, 32, 64) if v < n_aux] + [n_aux]
    nbuf = 4 if nu_blk >= 4 else nu_blk
    return pl.pallas_call(
        functools.partial(
            contract_kernel, n_aux, slots, aux_dev, pad, occ_local, nu_blk, levels
        ),
        out_shape=jax.ShapeDtypeStruct((occ_local, nu_local, aux_total), jnp.bfloat16),
        in_specs=[
            pl.BlockSpec(memory_space=pltpu.SMEM),
            pl.BlockSpec(memory_space=pltpu.VMEM),
            pl.BlockSpec(memory_space=pltpu.VMEM),
        ],
        out_specs=pl.BlockSpec(memory_space=pl.ANY),
        scratch_shapes=[
            pltpu.VMEM((n_aux * slots + 1, pad, lanes), jnp.bfloat16),
            pltpu.VMEM((n_aux * pad, lanes), jnp.bfloat16),
            pltpu.VMEM((n_aux * pad, aux_total), jnp.bfloat16),
            pltpu.VMEM((nbuf, occ_local, BLK, aux_total), jnp.bfloat16),
            pltpu.VMEM((occ_local, BLK, aux_total), jnp.bfloat16),
            pltpu.SemaphoreType.DMA((nbuf,)),
            pltpu.SMEM((nu_blk,), jnp.int32),
            pltpu.SMEM((nu_blk * n_aux,), jnp.int32),
        ],
        compiler_params=pltpu.CompilerParams(vmem_limit_bytes=40 * 1024 * 1024),
        name="contract_metric",
    )(nu_lists, recv, met)


def body(integrals, coefficients, metric, mu_blocks, nu_blocks, counts):
    n_aux = lax.axis_size("aux")
    aux_local, slots, _ = integrals.shape
    nbf = coefficients.shape[0] * lax.axis_size("orb")
    nu_local = nbf // lax.axis_size("orb")
    occ_total = coefficients.shape[1]
    occ_local = occ_total // n_aux
    aux_total = metric.shape[1]
    pad = -(-aux_local // 32) * 32

    nu = nu_blocks[0]
    live = jnp.arange(slots) < counts[0, 0]
    same = (nu[:, None] == nu[None, :]) & live[:, None] & live[None, :]
    first = live & ~jnp.any(jnp.tril(same, -1), axis=1)
    keep = same & first[:, None]
    nu_list = jnp.where(first, nu, -1)

    tail = jnp.zeros((pad - aux_local, aux_total), metric.dtype)
    tail = tail.at[0, :slots].set(nu_list.astype(metric.dtype))
    wide = lax.all_gather(jnp.concatenate([metric, tail], axis=0), "aux", axis=0)
    nu_lists = wide[:, aux_local, :slots].astype(jnp.int32).reshape(-1)
    met = wide[:, :aux_local].reshape(n_aux * aux_local, aux_total).T
    met = met.reshape(n_aux, aux_local, aux_total)
    met = jnp.pad(met, ((0, 0), (0, pad - aux_local), (0, 0)))

    coef_wide = lax.all_gather(coefficients, "orb", axis=0, tiled=True)
    rows = [
        lax.dynamic_slice_in_dim(coef_wide, mu_blocks[0, s] * BLK, BLK, 0)
        for s in range(slots)
    ]
    rows = jnp.stack(rows)
    coef = jnp.where(keep[:, :, None, None], rows[None], jnp.zeros_like(rows[None]))
    coef = coef.transpose(0, 3, 1, 2).reshape(slots * occ_total, slots * BLK)
    blocks = integrals.reshape(aux_local, slots, BLK, BLK).transpose(1, 2, 0, 3)
    half = jnp.dot(
        coef,
        blocks.reshape(slots * BLK, aux_local * BLK),
        preferred_element_type=jnp.float32,
    ).astype(jnp.bfloat16)
    half = half.reshape(slots, n_aux, occ_local, aux_local, BLK)
    msg = half.transpose(1, 0, 3, 2, 4).reshape(n_aux, slots * aux_local, occ_local * BLK)

    recv = exchange(msg, n_aux)
    return contract(nu_lists, recv, met, occ_local, nu_local)


def solution(mesh):
    placed = (
        P("aux", "orb", None),
        P("orb", None),
        P("aux", None),
        P("aux", "orb"),
        P("aux", "orb"),
        P("aux", "orb"),
    )
    return jax.shard_map(
        body, mesh=mesh, in_specs=placed, out_specs=P("aux", "orb", None), check_vma=False
    )
```

```python
import functools

import jax
import jax.numpy as jnp
from jax import lax
from jax.experimental import pallas as pl
from jax.experimental.pallas import tpu as pltpu
from jax.sharding import PartitionSpec as P

BLK = 64
MESH = pl.DeviceIdType.MESH


def mate_kernel(mine_ref, both_ref, send_sem, recv_sem, own_sem):
    aux = lax.axis_index("aux")
    orb = lax.axis_index("orb")
    barrier = pltpu.get_barrier_semaphore()
    pl.semaphore_signal(barrier, inc=1, device_id=(aux, 1 - orb), device_id_type=MESH)
    pl.semaphore_wait(barrier, 1)
    copy = pltpu.make_async_remote_copy(
        src_ref=mine_ref,
        dst_ref=both_ref.at[orb],
        send_sem=send_sem,
        recv_sem=recv_sem,
        device_id=(aux, 1 - orb),
        device_id_type=MESH,
    )
    copy.start()
    own = pltpu.make_async_copy(mine_ref, both_ref.at[orb], own_sem)
    own.start()
    own.wait()
    copy.wait_send()
    pltpu.make_async_remote_copy(
        src_ref=mine_ref,
        dst_ref=both_ref.at[1 - orb],
        send_sem=send_sem,
        recv_sem=recv_sem,
        device_id=(aux, 1 - orb),
        device_id_type=MESH,
    ).wait_recv()


def gather_coefficients(coefficients):
    if lax.axis_size("orb") != 2:
        return lax.all_gather(coefficients, "orb", axis=0, tiled=True)
    both = pl.pallas_call(
        mate_kernel,
        out_shape=jax.ShapeDtypeStruct((2,) + coefficients.shape, coefficients.dtype),
        in_specs=[pl.BlockSpec(memory_space=pl.ANY)],
        out_specs=pl.BlockSpec(memory_space=pl.ANY),
        scratch_shapes=[pltpu.SemaphoreType.DMA] * 3,
        compiler_params=pltpu.CompilerParams(collective_id=1, has_side_effects=True),
        name="mate_coefficients",
    )(coefficients)
    return both.reshape(-1, coefficients.shape[1])


def half_kernel(aux_dev, slots, n_aux, high, coef_ref, blocks_ref, msg_ref, rows_ref):
    def one(p, _):
        x = blocks_ref[p]
        z = jnp.zeros_like(x)
        wide = jnp.concatenate(
            [jnp.concatenate([x, z], axis=1), jnp.concatenate([z, x], axis=1)], axis=0
        )
        part = jnp.dot(coef_ref[...], wide, preferred_element_type=jnp.float32)
        rows_ref[pl.ds(p, part.shape[0], stride=aux_dev), :] = part
        return 0

    lax.fori_loop(0, aux_dev, one, 0, unroll=2)

    def pack(d, _):
        for i in range(high):
            parts = []
            for s in range(slots):
                at = ((s * n_aux + d) * high + i) * aux_dev
                parts.append(rows_ref[pl.ds(pl.multiple_of(at, 8), aux_dev), :])
            msg_ref[d, :, i * 128 : (i + 1) * 128] = jnp.concatenate(parts, axis=0).astype(
                msg_ref.dtype
            )
        return 0

    lax.fori_loop(0, n_aux, pack, 0)


def half_messages(coef, blocks, n_aux, slots, high):
    aux_dev = blocks.shape[0]
    return pl.pallas_call(
        functools.partial(half_kernel, aux_dev, slots, n_aux, high),
        out_shape=jax.ShapeDtypeStruct((n_aux, slots * aux_dev, high * 128), jnp.bfloat16),
        in_specs=[pl.BlockSpec(memory_space=pltpu.VMEM)] * 2,
        out_specs=pl.BlockSpec(memory_space=pltpu.VMEM),
        scratch_shapes=[pltpu.VMEM((coef.shape[0] * aux_dev, 128), jnp.float32)],
        compiler_params=pltpu.CompilerParams(vmem_limit_bytes=40 * 1024 * 1024),
        name="half_messages",
    )(coef, blocks)


def exchange_kernel(
    n, share, msg_ref, meta_ref, recv_ref, *rest
):
    metas_ref, mates_ref = rest[0], (rest[1] if share == 2 else None)
    send_sem, recv_sem, msend_sem, mrecv_sem, own_sem = rest[share:]
    me = lax.axis_index("aux")
    orb = lax.axis_index("orb")
    barrier = pltpu.get_barrier_semaphore()
    for k in range(1, n):
        pl.semaphore_signal(
            barrier, inc=1, device_id=(lax.rem(me + k, n), orb), device_id_type=MESH
        )
    if share == 2:
        pl.semaphore_signal(barrier, inc=1, device_id=(me, 1 - orb), device_id_type=MESH)
    pl.semaphore_wait(barrier, n - 1 + (share == 2))
    order = sorted(range(1, n), key=lambda k: abs(k - n // 2))

    def meta_copy(k, peer, slab):
        return pltpu.make_async_remote_copy(
            src_ref=meta_ref,
            dst_ref=metas_ref.at[slab],
            send_sem=msend_sem.at[k],
            recv_sem=mrecv_sem.at[k],
            device_id=(peer, orb),
            device_id_type=MESH,
        )

    def msg_copy(k, peer, slab):
        return pltpu.make_async_remote_copy(
            src_ref=msg_ref.at[peer],
            dst_ref=recv_ref.at[slab],
            send_sem=send_sem.at[k],
            recv_sem=recv_sem.at[k],
            device_id=(peer, orb),
            device_id_type=MESH,
        )

    for k in order:
        meta_copy(k, lax.rem(me + k, n), me).start()
    for k in order:
        msg_copy(k, lax.rem(me + k, n), me).start()
    own = pltpu.make_async_copy(msg_ref.at[me], recv_ref.at[me], own_sem.at[0])
    own.start()
    own_meta = pltpu.make_async_copy(meta_ref, metas_ref.at[me], own_sem.at[1])
    own_meta.start()
    own_meta.wait()
    for k in order:
        source = lax.rem(me - k + n, n)
        meta_copy(k, source, source).wait_recv()
    if share == 2:
        hand = pltpu.make_async_remote_copy(
            src_ref=metas_ref,
            dst_ref=mates_ref,
            send_sem=msend_sem.at[0],
            recv_sem=mrecv_sem.at[0],
            device_id=(me, 1 - orb),
            device_id_type=MESH,
        )
        hand.start()
        hand.wait()
    own.wait()
    for k in order:
        peer = lax.rem(me + k, n)
        source = lax.rem(me - k + n, n)
        meta_copy(k, peer, me).wait_send()
        msg_copy(k, peer, me).wait_send()
        msg_copy(k, source, source).wait_recv()


def exchange(msg, meta, n, share):
    metas = jax.ShapeDtypeStruct((n,) + meta.shape, meta.dtype)
    return pl.pallas_call(
        functools.partial(exchange_kernel, n, share),
        out_shape=[jax.ShapeDtypeStruct(msg.shape, msg.dtype)] + [metas] * share,
        in_specs=[pl.BlockSpec(memory_space=pl.ANY)] * 2,
        out_specs=[pl.BlockSpec(memory_space=pl.ANY)] * (1 + share),
        scratch_shapes=[pltpu.SemaphoreType.DMA((n,))] * 4 + [pltpu.SemaphoreType.DMA((2,))],
        compiler_params=pltpu.CompilerParams(collective_id=0, has_side_effects=True),
        name="exchange_slots",
    )(msg, meta)


def contract_kernel(
    n_aux, slots, aux_dev, pad, occ_local, nu_blk, levels,
    nu_ref, recv_ref, met_ref, out_ref,
    held, padded, lhs, wgt, obuf, zero, sems, zsems, lsem, count, lists,
):
    total = n_aux * slots
    lanes = occ_local * BLK
    aux_total = out_ref.shape[2]

    def clear(b, _):
        count[b] = 0
        return 0

    lax.fori_loop(0, nu_blk, clear, 0)

    def enlist(e, _):
        b = nu_ref[e]

        @pl.when(b >= 0)
        def _():
            c = count[b]
            lists[b * n_aux + c] = e
            count[b] = c + 1

        return 0

    lax.fori_loop(0, total, enlist, 0)

    def out_copy(src, b, sem):
        return pltpu.make_async_copy(
            src, out_ref.at[:, pl.ds(pl.multiple_of(b * BLK, BLK), BLK), :], sem
        )

    load = pltpu.make_async_copy(recv_ref, held, lsem)
    load.start()
    zero[...] = jnp.zeros_like(zero)

    def empty(b, _):
        @pl.when(count[b] == 0)
        def _():
            out_copy(zero, b, zsems.at[b]).start()

        return 0

    lax.fori_loop(0, nu_blk, empty, 0)
    padded[total] = jnp.zeros((pad, lanes), padded.dtype)
    load.wait()

    def spread(a, _):
        rows = held[a]
        for s in range(slots):
            part = rows[s * aux_dev : (s + 1) * aux_dev]
            padded[a * slots + s] = jnp.concatenate(
                [part, jnp.zeros((pad - aux_dev, lanes), part.dtype)], axis=0
            )
        return 0

    lax.fori_loop(0, n_aux, spread, 0)
    nbuf = obuf.shape[0]
    high = occ_local // 2

    def block(b, used):
        c = count[b]
        which = lax.rem(used, nbuf)

        @pl.when((c > 0) & (used >= nbuf))
        def _():
            out_copy(obuf.at[which], b, sems.at[which]).wait()

        low = 0
        for level in levels:

            @pl.when((c > low) & (c <= level))
            def _(level=level):
                for j in range(level):
                    e = jnp.where(j < c, lists[b * n_aux + jnp.minimum(j, c - 1)], total)
                    a = jnp.where(j < c, e // slots, 0)
                    lhs[j * pad : (j + 1) * pad, :] = padded[e]
                    wgt[j * pad : (j + 1) * pad, :] = met_ref[a]
                depth = level * pad
                for i in range(high):
                    res = lax.dot_general(
                        lhs[:depth, i * 128 : (i + 1) * 128],
                        wgt[:depth, :],
                        (((0,), (0,)), ((), ())),
                        preferred_element_type=jnp.float32,
                    ).astype(obuf.dtype)
                    obuf[which, i] = res[:BLK]
                    obuf[which, i + high] = res[BLK:]
                out_copy(obuf.at[which], b, sems.at[which]).start()

            low = level
        return jnp.where(c > 0, used + 1, used)

    used = lax.fori_loop(0, nu_blk, block, 0)
    for w in range(nbuf):

        @pl.when(used > w)
        def _():
            out_copy(obuf.at[w], 0, sems.at[w]).wait()

    def drain(b, _):
        @pl.when(count[b] == 0)
        def _():
            out_copy(zero, b, zsems.at[b]).wait()

        return 0

    lax.fori_loop(0, nu_blk, drain, 0)


def contract(nu_lists, recv, met, occ_local, nu_local):
    n_aux, rows, lanes = recv.shape
    slots = nu_lists.shape[0] // n_aux
    aux_dev = rows // slots
    pad = met.shape[1]
    aux_total = met.shape[2]
    nu_blk = nu_local // BLK
    levels = [v for v in (1, 2, 4, 8, 16, 32, 64) if v < n_aux] + [n_aux]
    nbuf = 4 if nu_blk >= 4 else nu_blk
    return pl.pallas_call(
        functools.partial(
            contract_kernel, n_aux, slots, aux_dev, pad, occ_local, nu_blk, levels
        ),
        out_shape=jax.ShapeDtypeStruct((occ_local, nu_local, aux_total), jnp.bfloat16),
        in_specs=[
            pl.BlockSpec(memory_space=pltpu.SMEM),
            pl.BlockSpec(memory_space=pl.ANY),
            pl.BlockSpec(memory_space=pltpu.VMEM),
        ],
        out_specs=pl.BlockSpec(memory_space=pl.ANY),
        scratch_shapes=[
            pltpu.VMEM(recv.shape, jnp.bfloat16),
            pltpu.VMEM((n_aux * slots + 1, pad, lanes), jnp.bfloat16),
            pltpu.VMEM((n_aux * pad, lanes), jnp.bfloat16),
            pltpu.VMEM((n_aux * pad, aux_total), jnp.bfloat16),
            pltpu.VMEM((nbuf, occ_local, BLK, aux_total), jnp.bfloat16),
            pltpu.VMEM((occ_local, BLK, aux_total), jnp.bfloat16),
            pltpu.SemaphoreType.DMA((nbuf,)),
            pltpu.SemaphoreType.DMA((nu_blk,)),
            pltpu.SemaphoreType.DMA,
            pltpu.SMEM((nu_blk,), jnp.int32),
            pltpu.SMEM((nu_blk * n_aux,), jnp.int32),
        ],
        compiler_params=pltpu.CompilerParams(vmem_limit_bytes=40 * 1024 * 1024),
        name="contract_metric",
    )(nu_lists, recv, met)


def body(integrals, coefficients, metric, mu_blocks, nu_blocks, counts):
    n_aux = lax.axis_size("aux")
    aux_local, slots, _ = integrals.shape
    nbf = coefficients.shape[0] * lax.axis_size("orb")
    nu_local = nbf // lax.axis_size("orb")
    occ_total = coefficients.shape[1]
    occ_local = occ_total // n_aux
    aux_total = metric.shape[1]
    pad = -(-aux_local // 32) * 32

    nu = nu_blocks[0]
    live = jnp.arange(slots) < counts[0, 0]
    same = (nu[:, None] == nu[None, :]) & live[:, None] & live[None, :]
    first = live & ~jnp.any(jnp.tril(same, -1), axis=1)
    keep = same & first[:, None]
    nu_list = jnp.where(first, nu, -1)

    orb = lax.axis_index("orb")
    share = 2 if lax.axis_size("orb") == 2 else 1
    part = aux_local // share
    tall = -(-(part + 1) // 16) * 16
    own_rows = lax.dynamic_slice_in_dim(metric, orb * part if share == 2 else 0, part, 0)
    tail = jnp.zeros((tall - part, aux_total), metric.dtype)
    tail = tail.at[0, :slots].set(nu_list.astype(metric.dtype))
    meta = jnp.concatenate([own_rows, tail], axis=0)

    coef_wide = gather_coefficients(coefficients)
    rows = jnp.stack(
        [
            lax.dynamic_slice_in_dim(coef_wide, mu_blocks[0, s] * BLK, BLK, 0)
            for s in range(slots)
        ]
    )
    high = occ_local // 2
    coef = rows.reshape(slots, BLK, n_aux, 2, high).transpose(2, 4, 3, 0, 1)
    coef = coef.reshape(1, n_aux * high, 2, slots, BLK)
    coef = jnp.where(keep[:, None, None, :, None], coef, jnp.zeros_like(coef))
    coef = coef.reshape(slots * n_aux * high, 2 * slots * BLK)
    blocks = integrals.reshape(aux_local, slots * BLK, BLK)
    msg = half_messages(coef, blocks, n_aux, slots, high)

    recv, *metas = exchange(msg, meta, n_aux, share)
    nu_lists = metas[0][:, part, :slots].astype(jnp.int32).reshape(-1)
    if share == 2:
        swap = orb == 1
        first_rows = jnp.where(swap, metas[1], metas[0])
        second_rows = jnp.where(swap, metas[0], metas[1])
        wide = jnp.concatenate([first_rows[:, :part], second_rows[:, :part]], axis=1)
    else:
        wide = metas[0][:, :part]
    met = wide.reshape(n_aux * aux_local, aux_total).T
    met = met.reshape(n_aux, aux_local, aux_total)
    met = jnp.pad(met, ((0, 0), (0, pad - aux_local), (0, 0)))
    return contract(nu_lists, recv, met, occ_local, nu_local)


def solution(mesh):
    placed = (
        P("aux", "orb", None),
        P("orb", None),
        P("aux", None),
        P("aux", "orb"),
        P("aux", "orb"),
        P("aux", "orb"),
    )
    return jax.shard_map(
        body, mesh=mesh, in_specs=placed, out_specs=P("aux", "orb", None), check_vma=False
    )
```

```python
import functools

import jax
import jax.numpy as jnp
from jax import lax
from jax.experimental import pallas as pl
from jax.experimental.pallas import tpu as pltpu
from jax.sharding import PartitionSpec as P

BLK = 64
MESH = pl.DeviceIdType.MESH


def mate_kernel(mine_ref, both_ref, send_sem, recv_sem, own_sem):
    aux = lax.axis_index("aux")
    orb = lax.axis_index("orb")
    barrier = pltpu.get_barrier_semaphore()
    pl.semaphore_signal(barrier, inc=1, device_id=(aux, 1 - orb), device_id_type=MESH)
    pl.semaphore_wait(barrier, 1)
    copy = pltpu.make_async_remote_copy(
        src_ref=mine_ref,
        dst_ref=both_ref.at[orb],
        send_sem=send_sem,
        recv_sem=recv_sem,
        device_id=(aux, 1 - orb),
        device_id_type=MESH,
    )
    copy.start()
    own = pltpu.make_async_copy(mine_ref, both_ref.at[orb], own_sem)
    own.start()
    own.wait()
    copy.wait_send()
    pltpu.make_async_remote_copy(
        src_ref=mine_ref,
        dst_ref=both_ref.at[1 - orb],
        send_sem=send_sem,
        recv_sem=recv_sem,
        device_id=(aux, 1 - orb),
        device_id_type=MESH,
    ).wait_recv()


def swap_mates(mine, collective_id, name):
    return pl.pallas_call(
        mate_kernel,
        out_shape=jax.ShapeDtypeStruct((2,) + mine.shape, mine.dtype),
        in_specs=[pl.BlockSpec(memory_space=pltpu.VMEM)],
        out_specs=pl.BlockSpec(memory_space=pltpu.VMEM),
        scratch_shapes=[pltpu.SemaphoreType.DMA] * 3,
        compiler_params=pltpu.CompilerParams(
            collective_id=collective_id, has_side_effects=True
        ),
        name=name,
    )(mine)


def arrange(rows, n_aux, high):
    slots = rows.shape[0]
    rows = rows.reshape(slots, BLK, n_aux, 2, high).transpose(2, 4, 3, 0, 1)
    return rows.reshape(n_aux * high, 2 * slots * BLK)


def listed_coefficients(coefficients, mu, n_aux, high):
    slots = mu.shape[0]

    def pick(source, at):
        return jnp.stack(
            [lax.dynamic_slice_in_dim(source, at[s] * BLK, BLK, 0) for s in range(slots)]
        )

    if lax.axis_size("orb") != 2:
        wide = lax.all_gather(coefficients, "orb", axis=0, tiled=True)
        return arrange(pick(wide, mu), n_aux, high)
    orb = lax.axis_index("orb")
    held = coefficients.shape[0] // BLK
    asked = jnp.zeros((8, 128), jnp.int32).at[0, :slots].set(mu)
    asked = swap_mates(asked, 1, "swap_lists")[:, 0, :slots]
    mates = jnp.where(orb == 0, asked[1], asked[0])

    def from_own(at):
        near = at - orb * held
        return arrange(pick(coefficients, jnp.clip(near, 0, held - 1)), n_aux, high)

    given = swap_mates(from_own(mates), 2, "swap_rows")
    given = jnp.where(orb == 0, given[1], given[0])
    mine = from_own(mu)
    near = mu // held == orb
    shape = (n_aux * high, 2, slots, BLK)
    merged = jnp.where(
        near[None, None, :, None], mine.reshape(shape), given.reshape(shape)
    )
    return merged.reshape(mine.shape)


def half_kernel(aux_dev, slots, n_aux, high, coef_ref, blocks_ref, msg_ref, rows_ref):
    def one(p, _):
        x = blocks_ref[p]
        z = jnp.zeros_like(x)
        wide = jnp.concatenate(
            [jnp.concatenate([x, z], axis=1), jnp.concatenate([z, x], axis=1)], axis=0
        )
        part = jnp.dot(coef_ref[...], wide, preferred_element_type=jnp.float32)
        rows_ref[pl.ds(p, part.shape[0], stride=aux_dev), :] = part
        return 0

    lax.fori_loop(0, aux_dev, one, 0, unroll=2)

    def pack(d, _):
        for i in range(high):
            parts = []
            for s in range(slots):
                at = ((s * n_aux + d) * high + i) * aux_dev
                parts.append(rows_ref[pl.ds(pl.multiple_of(at, 8), aux_dev), :])
            msg_ref[d, :, i * 128 : (i + 1) * 128] = jnp.concatenate(parts, axis=0).astype(
                msg_ref.dtype
            )
        return 0

    lax.fori_loop(0, n_aux, pack, 0)


def half_messages(coef, blocks, n_aux, slots, high):
    aux_dev = blocks.shape[0]
    return pl.pallas_call(
        functools.partial(half_kernel, aux_dev, slots, n_aux, high),
        out_shape=jax.ShapeDtypeStruct((n_aux, slots * aux_dev, high * 128), jnp.bfloat16),
        in_specs=[pl.BlockSpec(memory_space=pltpu.VMEM)] * 2,
        out_specs=pl.BlockSpec(memory_space=pltpu.VMEM),
        scratch_shapes=[pltpu.VMEM((coef.shape[0] * aux_dev, 128), jnp.float32)],
        compiler_params=pltpu.CompilerParams(vmem_limit_bytes=40 * 1024 * 1024),
        name="half_messages",
    )(coef, blocks)


def exchange_kernel(
    n, share, msg_ref, meta_ref, recv_ref, *rest
):
    metas_ref, mates_ref = rest[0], (rest[1] if share == 2 else None)
    send_sem, recv_sem, msend_sem, mrecv_sem, own_sem = rest[share:]
    me = lax.axis_index("aux")
    orb = lax.axis_index("orb")
    barrier = pltpu.get_barrier_semaphore()
    for k in range(1, n):
        pl.semaphore_signal(
            barrier, inc=1, device_id=(lax.rem(me + k, n), orb), device_id_type=MESH
        )
    if share == 2:
        pl.semaphore_signal(barrier, inc=1, device_id=(me, 1 - orb), device_id_type=MESH)
    pl.semaphore_wait(barrier, n - 1 + (share == 2))
    order = sorted(range(1, n), key=lambda k: abs(k - n // 2))

    def meta_copy(k, peer, slab):
        return pltpu.make_async_remote_copy(
            src_ref=meta_ref,
            dst_ref=metas_ref.at[slab],
            send_sem=msend_sem.at[k],
            recv_sem=mrecv_sem.at[k],
            device_id=(peer, orb),
            device_id_type=MESH,
        )

    def msg_copy(k, peer, slab):
        return pltpu.make_async_remote_copy(
            src_ref=msg_ref.at[peer],
            dst_ref=recv_ref.at[slab],
            send_sem=send_sem.at[k],
            recv_sem=recv_sem.at[k],
            device_id=(peer, orb),
            device_id_type=MESH,
        )

    for k in order:
        meta_copy(k, lax.rem(me + k, n), me).start()
    for k in order:
        msg_copy(k, lax.rem(me + k, n), me).start()
    own = pltpu.make_async_copy(msg_ref.at[me], recv_ref.at[me], own_sem.at[0])
    own.start()
    own_meta = pltpu.make_async_copy(meta_ref, metas_ref.at[me], own_sem.at[1])
    own_meta.start()
    own_meta.wait()
    for k in order:
        source = lax.rem(me - k + n, n)
        meta_copy(k, source, source).wait_recv()
    if share == 2:
        hand = pltpu.make_async_remote_copy(
            src_ref=metas_ref,
            dst_ref=mates_ref,
            send_sem=msend_sem.at[0],
            recv_sem=mrecv_sem.at[0],
            device_id=(me, 1 - orb),
            device_id_type=MESH,
        )
        hand.start()
        hand.wait()
    own.wait()
    for k in order:
        peer = lax.rem(me + k, n)
        source = lax.rem(me - k + n, n)
        meta_copy(k, peer, me).wait_send()
        msg_copy(k, peer, me).wait_send()
        msg_copy(k, source, source).wait_recv()


def exchange(msg, meta, n, share):
    metas = jax.ShapeDtypeStruct((n,) + meta.shape, meta.dtype)
    return pl.pallas_call(
        functools.partial(exchange_kernel, n, share),
        out_shape=[jax.ShapeDtypeStruct(msg.shape, msg.dtype)] + [metas] * share,
        in_specs=[pl.BlockSpec(memory_space=pl.ANY)] * 2,
        out_specs=[pl.BlockSpec(memory_space=pl.ANY)] * (1 + share),
        scratch_shapes=[pltpu.SemaphoreType.DMA((n,))] * 4 + [pltpu.SemaphoreType.DMA((2,))],
        compiler_params=pltpu.CompilerParams(collective_id=0, has_side_effects=True),
        name="exchange_slots",
    )(msg, meta)


def contract_kernel(
    n_aux, slots, aux_dev, pad, occ_local, nu_blk, levels,
    nu_ref, recv_ref, met_ref, out_ref,
    held, padded, lhs, wgt, obuf, zero, sems, zsems, lsem, count, lists,
):
    total = n_aux * slots
    lanes = occ_local * BLK
    aux_total = out_ref.shape[2]

    def clear(b, _):
        count[b] = 0
        return 0

    lax.fori_loop(0, nu_blk, clear, 0)

    def enlist(e, _):
        b = nu_ref[e]

        @pl.when(b >= 0)
        def _():
            c = count[b]
            lists[b * n_aux + c] = e
            count[b] = c + 1

        return 0

    lax.fori_loop(0, total, enlist, 0)

    def out_copy(src, b, sem):
        return pltpu.make_async_copy(
            src, out_ref.at[:, pl.ds(pl.multiple_of(b * BLK, BLK), BLK), :], sem
        )

    load = pltpu.make_async_copy(recv_ref, held, lsem)
    load.start()
    zero[...] = jnp.zeros_like(zero)

    def empty(b, _):
        @pl.when(count[b] == 0)
        def _():
            out_copy(zero, b, zsems.at[b]).start()

        return 0

    lax.fori_loop(0, nu_blk, empty, 0)
    padded[total] = jnp.zeros((pad, lanes), padded.dtype)
    load.wait()

    def spread(a, _):
        rows = held[a]
        for s in range(slots):
            part = rows[s * aux_dev : (s + 1) * aux_dev]
            padded[a * slots + s] = jnp.concatenate(
                [part, jnp.zeros((pad - aux_dev, lanes), part.dtype)], axis=0
            )
        return 0

    lax.fori_loop(0, n_aux, spread, 0)
    nbuf = obuf.shape[0]
    high = occ_local // 2

    def block(b, used):
        c = count[b]
        which = lax.rem(used, nbuf)

        @pl.when((c > 0) & (used >= nbuf))
        def _():
            out_copy(obuf.at[which], b, sems.at[which]).wait()

        low = 0
        for level in levels:

            @pl.when((c > low) & (c <= level))
            def _(level=level):
                for j in range(level):
                    e = jnp.where(j < c, lists[b * n_aux + jnp.minimum(j, c - 1)], total)
                    a = jnp.where(j < c, e // slots, 0)
                    lhs[j * pad : (j + 1) * pad, :] = padded[e]
                    wgt[j * pad : (j + 1) * pad, :] = met_ref[a]
                depth = level * pad
                for i in range(high):
                    res = lax.dot_general(
                        lhs[:depth, i * 128 : (i + 1) * 128],
                        wgt[:depth, :],
                        (((0,), (0,)), ((), ())),
                        preferred_element_type=jnp.float32,
                    ).astype(obuf.dtype)
                    obuf[which, i] = res[:BLK]
                    obuf[which, i + high] = res[BLK:]
                out_copy(obuf.at[which], b, sems.at[which]).start()

            low = level
        return jnp.where(c > 0, used + 1, used)

    used = lax.fori_loop(0, nu_blk, block, 0)
    for w in range(nbuf):

        @pl.when(used > w)
        def _():
            out_copy(obuf.at[w], 0, sems.at[w]).wait()

    def drain(b, _):
        @pl.when(count[b] == 0)
        def _():
            out_copy(zero, b, zsems.at[b]).wait()

        return 0

    lax.fori_loop(0, nu_blk, drain, 0)


def contract(nu_lists, recv, met, occ_local, nu_local):
    n_aux, rows, lanes = recv.shape
    slots = nu_lists.shape[0] // n_aux
    aux_dev = rows // slots
    pad = met.shape[1]
    aux_total = met.shape[2]
    nu_blk = nu_local // BLK
    levels = [v for v in (1, 2, 4, 8, 16, 32, 64) if v < n_aux] + [n_aux]
    nbuf = 4 if nu_blk >= 4 else nu_blk
    return pl.pallas_call(
        functools.partial(
            contract_kernel, n_aux, slots, aux_dev, pad, occ_local, nu_blk, levels
        ),
        out_shape=jax.ShapeDtypeStruct((occ_local, nu_local, aux_total), jnp.bfloat16),
        in_specs=[
            pl.BlockSpec(memory_space=pltpu.SMEM),
            pl.BlockSpec(memory_space=pl.ANY),
            pl.BlockSpec(memory_space=pltpu.VMEM),
        ],
        out_specs=pl.BlockSpec(memory_space=pl.ANY),
        scratch_shapes=[
            pltpu.VMEM(recv.shape, jnp.bfloat16),
            pltpu.VMEM((n_aux * slots + 1, pad, lanes), jnp.bfloat16),
            pltpu.VMEM((n_aux * pad, lanes), jnp.bfloat16),
            pltpu.VMEM((n_aux * pad, aux_total), jnp.bfloat16),
            pltpu.VMEM((nbuf, occ_local, BLK, aux_total), jnp.bfloat16),
            pltpu.VMEM((occ_local, BLK, aux_total), jnp.bfloat16),
            pltpu.SemaphoreType.DMA((nbuf,)),
            pltpu.SemaphoreType.DMA((nu_blk,)),
            pltpu.SemaphoreType.DMA,
            pltpu.SMEM((nu_blk,), jnp.int32),
            pltpu.SMEM((nu_blk * n_aux,), jnp.int32),
        ],
        compiler_params=pltpu.CompilerParams(vmem_limit_bytes=40 * 1024 * 1024),
        name="contract_metric",
    )(nu_lists, recv, met)


def body(integrals, coefficients, metric, mu_blocks, nu_blocks, counts):
    n_aux = lax.axis_size("aux")
    aux_local, slots, _ = integrals.shape
    nbf = coefficients.shape[0] * lax.axis_size("orb")
    nu_local = nbf // lax.axis_size("orb")
    occ_total = coefficients.shape[1]
    occ_local = occ_total // n_aux
    aux_total = metric.shape[1]
    pad = -(-aux_local // 32) * 32

    nu = nu_blocks[0]
    live = jnp.arange(slots) < counts[0, 0]
    same = (nu[:, None] == nu[None, :]) & live[:, None] & live[None, :]
    first = live & ~jnp.any(jnp.tril(same, -1), axis=1)
    keep = same & first[:, None]
    nu_list = jnp.where(first, nu, -1)

    orb = lax.axis_index("orb")
    share = 2 if lax.axis_size("orb") == 2 else 1
    part = aux_local // share
    tall = -(-(part + 1) // 16) * 16
    own_rows = lax.dynamic_slice_in_dim(metric, orb * part if share == 2 else 0, part, 0)
    tail = jnp.zeros((tall - part, aux_total), metric.dtype)
    tail = tail.at[0, :slots].set(nu_list.astype(metric.dtype))
    meta = jnp.concatenate([own_rows, tail], axis=0)

    high = occ_local // 2
    coef = listed_coefficients(coefficients, mu_blocks[0], n_aux, high)
    coef = coef.reshape(1, n_aux * high, 2, slots, BLK)
    coef = jnp.where(keep[:, None, None, :, None], coef, jnp.zeros_like(coef))
    coef = coef.reshape(slots * n_aux * high, 2 * slots * BLK)
    blocks = integrals.reshape(aux_local, slots * BLK, BLK)
    msg = half_messages(coef, blocks, n_aux, slots, high)

    recv, *metas = exchange(msg, meta, n_aux, share)
    nu_lists = metas[0][:, part, :slots].astype(jnp.int32).reshape(-1)
    if share == 2:
        swap = orb == 1
        first_rows = jnp.where(swap, metas[1], metas[0])
        second_rows = jnp.where(swap, metas[0], metas[1])
        wide = jnp.concatenate([first_rows[:, :part], second_rows[:, :part]], axis=1)
    else:
        wide = metas[0][:, :part]
    met = wide.reshape(n_aux * aux_local, aux_total).T
    met = met.reshape(n_aux, aux_local, aux_total)
    met = jnp.pad(met, ((0, 0), (0, pad - aux_local), (0, 0)))
    return contract(nu_lists, recv, met, occ_local, nu_local)


def solution(mesh):
    placed = (
        P("aux", "orb", None),
        P("orb", None),
        P("aux", None),
        P("aux", "orb"),
        P("aux", "orb"),
        P("aux", "orb"),
    )
    return jax.shard_map(
        body, mesh=mesh, in_specs=placed, out_specs=P("aux", "orb", None), check_vma=False
    )
```

```python
import functools

import jax
import jax.numpy as jnp
from jax import lax
from jax.experimental import pallas as pl
from jax.experimental.pallas import tpu as pltpu
from jax.sharding import PartitionSpec as P

BLK = 64
MESH = pl.DeviceIdType.MESH


def mate_kernel(mine_ref, both_ref, send_sem, recv_sem, own_sem):
    aux = lax.axis_index("aux")
    orb = lax.axis_index("orb")
    barrier = pltpu.get_barrier_semaphore()
    pl.semaphore_signal(barrier, inc=1, device_id=(aux, 1 - orb), device_id_type=MESH)
    pl.semaphore_wait(barrier, 1)
    copy = pltpu.make_async_remote_copy(
        src_ref=mine_ref,
        dst_ref=both_ref.at[orb],
        send_sem=send_sem,
        recv_sem=recv_sem,
        device_id=(aux, 1 - orb),
        device_id_type=MESH,
    )
    copy.start()
    own = pltpu.make_async_copy(mine_ref, both_ref.at[orb], own_sem)
    own.start()
    own.wait()
    copy.wait_send()
    pltpu.make_async_remote_copy(
        src_ref=mine_ref,
        dst_ref=both_ref.at[1 - orb],
        send_sem=send_sem,
        recv_sem=recv_sem,
        device_id=(aux, 1 - orb),
        device_id_type=MESH,
    ).wait_recv()


def swap_mates(mine, collective_id, name):
    return pl.pallas_call(
        mate_kernel,
        out_shape=jax.ShapeDtypeStruct((2,) + mine.shape, mine.dtype),
        in_specs=[pl.BlockSpec(memory_space=pltpu.VMEM)],
        out_specs=pl.BlockSpec(memory_space=pltpu.VMEM),
        scratch_shapes=[pltpu.SemaphoreType.DMA] * 3,
        compiler_params=pltpu.CompilerParams(
            collective_id=collective_id, has_side_effects=True
        ),
        name=name,
    )(mine)


def arrange(rows, n_aux, high):
    slots = rows.shape[0]
    rows = rows.reshape(slots, BLK, n_aux, 2, high).transpose(2, 4, 3, 0, 1)
    return rows.reshape(n_aux * high, 2 * slots * BLK)


def listed_coefficients(coefficients, mu, n_aux, high):
    slots = mu.shape[0]

    def pick(source, at):
        return jnp.stack(
            [lax.dynamic_slice_in_dim(source, at[s] * BLK, BLK, 0) for s in range(slots)]
        )

    if lax.axis_size("orb") != 2:
        wide = lax.all_gather(coefficients, "orb", axis=0, tiled=True)
        return arrange(pick(wide, mu), n_aux, high)
    orb = lax.axis_index("orb")
    held = coefficients.shape[0] // BLK
    asked = jnp.pad(mu[None], ((0, 7), (0, 128 - slots)))
    asked = swap_mates(asked, 1, "swap_lists")[:, 0, :slots]
    mates = jnp.where(orb == 0, asked[1], asked[0])

    def from_own(at):
        near = at - orb * held
        return arrange(pick(coefficients, jnp.clip(near, 0, held - 1)), n_aux, high)

    given = swap_mates(from_own(mates), 2, "swap_rows")
    given = jnp.where(orb == 0, given[1], given[0])
    mine = from_own(mu)
    near = mu // held == orb
    shape = (n_aux * high, 2, slots, BLK)
    merged = jnp.where(
        near[None, None, :, None], mine.reshape(shape), given.reshape(shape)
    )
    return merged.reshape(mine.shape)


def half_kernel(aux_dev, slots, n_aux, high, coef_ref, blocks_ref, msg_ref, rows_ref):
    def one(p, _):
        x = blocks_ref[p]
        z = jnp.zeros_like(x)
        wide = jnp.concatenate(
            [jnp.concatenate([x, z], axis=1), jnp.concatenate([z, x], axis=1)], axis=0
        )
        part = jnp.dot(coef_ref[...], wide, preferred_element_type=jnp.float32)
        rows_ref[pl.ds(p, part.shape[0], stride=aux_dev), :] = part
        return 0

    lax.fori_loop(0, aux_dev, one, 0, unroll=2)

    def pack(d, _):
        for i in range(high):
            parts = []
            for s in range(slots):
                at = ((s * n_aux + d) * high + i) * aux_dev
                parts.append(rows_ref[pl.ds(pl.multiple_of(at, 8), aux_dev), :])
            msg_ref[d, :, i * 128 : (i + 1) * 128] = jnp.concatenate(parts, axis=0).astype(
                msg_ref.dtype
            )
        return 0

    lax.fori_loop(0, n_aux, pack, 0)


def half_messages(coef, blocks, n_aux, slots, high):
    aux_dev = blocks.shape[0]
    return pl.pallas_call(
        functools.partial(half_kernel, aux_dev, slots, n_aux, high),
        out_shape=jax.ShapeDtypeStruct((n_aux, slots * aux_dev, high * 128), jnp.bfloat16),
        in_specs=[pl.BlockSpec(memory_space=pltpu.VMEM)] * 2,
        out_specs=pl.BlockSpec(memory_space=pltpu.VMEM),
        scratch_shapes=[pltpu.VMEM((coef.shape[0] * aux_dev, 128), jnp.float32)],
        compiler_params=pltpu.CompilerParams(vmem_limit_bytes=40 * 1024 * 1024),
        name="half_messages",
    )(coef, blocks)


def exchange_kernel(
    n, share, msg_ref, meta_ref, recv_ref, *rest
):
    metas_ref, mates_ref = rest[0], (rest[1] if share == 2 else None)
    send_sem, recv_sem, msend_sem, mrecv_sem, own_sem = rest[share:]
    me = lax.axis_index("aux")
    orb = lax.axis_index("orb")
    barrier = pltpu.get_barrier_semaphore()
    for k in range(1, n):
        pl.semaphore_signal(
            barrier, inc=1, device_id=(lax.rem(me + k, n), orb), device_id_type=MESH
        )
    if share == 2:
        pl.semaphore_signal(barrier, inc=1, device_id=(me, 1 - orb), device_id_type=MESH)
    pl.semaphore_wait(barrier, n - 1 + (share == 2))
    by_distance = sorted(range(1, n), key=lambda k: abs(k - n // 2))
    order = []
    while by_distance:
        order.append(by_distance.pop(0))
        if by_distance:
            order.append(by_distance.pop())

    def meta_copy(k, peer, slab):
        return pltpu.make_async_remote_copy(
            src_ref=meta_ref,
            dst_ref=metas_ref.at[slab],
            send_sem=msend_sem.at[k],
            recv_sem=mrecv_sem.at[k],
            device_id=(peer, orb),
            device_id_type=MESH,
        )

    def msg_copy(k, peer, slab):
        return pltpu.make_async_remote_copy(
            src_ref=msg_ref.at[peer],
            dst_ref=recv_ref.at[slab],
            send_sem=send_sem.at[k],
            recv_sem=recv_sem.at[k],
            device_id=(peer, orb),
            device_id_type=MESH,
        )

    for k in order:
        meta_copy(k, lax.rem(me + k, n), me).start()
    for k in order:
        msg_copy(k, lax.rem(me + k, n), me).start()
    own = pltpu.make_async_copy(msg_ref.at[me], recv_ref.at[me], own_sem.at[0])
    own.start()
    own_meta = pltpu.make_async_copy(meta_ref, metas_ref.at[me], own_sem.at[1])
    own_meta.start()
    own_meta.wait()
    for k in order:
        source = lax.rem(me - k + n, n)
        meta_copy(k, source, source).wait_recv()
    if share == 2:
        hand = pltpu.make_async_remote_copy(
            src_ref=metas_ref,
            dst_ref=mates_ref,
            send_sem=msend_sem.at[0],
            recv_sem=mrecv_sem.at[0],
            device_id=(me, 1 - orb),
            device_id_type=MESH,
        )
        hand.start()
        hand.wait()
    own.wait()
    for k in order:
        peer = lax.rem(me + k, n)
        source = lax.rem(me - k + n, n)
        meta_copy(k, peer, me).wait_send()
        msg_copy(k, peer, me).wait_send()
        msg_copy(k, source, source).wait_recv()


def exchange(msg, meta, n, share):
    metas = jax.ShapeDtypeStruct((n,) + meta.shape, meta.dtype)
    return pl.pallas_call(
        functools.partial(exchange_kernel, n, share),
        out_shape=[jax.ShapeDtypeStruct(msg.shape, msg.dtype)] + [metas] * share,
        in_specs=[pl.BlockSpec(memory_space=pl.ANY)] * 2,
        out_specs=[pl.BlockSpec(memory_space=pl.ANY)] * (1 + share),
        scratch_shapes=[pltpu.SemaphoreType.DMA((n,))] * 4 + [pltpu.SemaphoreType.DMA((2,))],
        compiler_params=pltpu.CompilerParams(collective_id=0, has_side_effects=True),
        name="exchange_slots",
    )(msg, meta)


def contract_kernel(
    n_aux, slots, aux_dev, pad, occ_local, nu_blk, levels,
    nu_ref, recv_ref, met_ref, out_ref,
    held, padded, lhs, wgt, obuf, zero, sems, zsems, lsem, count, lists,
):
    total = n_aux * slots
    lanes = occ_local * BLK
    aux_total = out_ref.shape[2]

    def clear(b, _):
        count[b] = 0
        return 0

    lax.fori_loop(0, nu_blk, clear, 0)

    def enlist(e, _):
        b = nu_ref[e]

        @pl.when(b >= 0)
        def _():
            c = count[b]
            lists[b * n_aux + c] = e
            count[b] = c + 1

        return 0

    lax.fori_loop(0, total, enlist, 0)

    def out_copy(src, b, sem):
        return pltpu.make_async_copy(
            src, out_ref.at[:, pl.ds(pl.multiple_of(b * BLK, BLK), BLK), :], sem
        )

    load = pltpu.make_async_copy(recv_ref, held, lsem)
    load.start()
    zero[...] = jnp.zeros_like(zero)

    def empty(b, _):
        @pl.when(count[b] == 0)
        def _():
            out_copy(zero, b, zsems.at[b]).start()

        return 0

    lax.fori_loop(0, nu_blk, empty, 0)
    padded[total] = jnp.zeros((pad, lanes), padded.dtype)
    load.wait()

    def spread(a, _):
        rows = held[a]
        for s in range(slots):
            part = rows[s * aux_dev : (s + 1) * aux_dev]
            padded[a * slots + s] = jnp.concatenate(
                [part, jnp.zeros((pad - aux_dev, lanes), part.dtype)], axis=0
            )
        return 0

    lax.fori_loop(0, n_aux, spread, 0)
    nbuf = obuf.shape[0]
    high = occ_local // 2

    def block(b, used):
        c = count[b]
        which = lax.rem(used, nbuf)

        @pl.when((c > 0) & (used >= nbuf))
        def _():
            out_copy(obuf.at[which], b, sems.at[which]).wait()

        low = 0
        for level in levels:

            @pl.when((c > low) & (c <= level))
            def _(level=level):
                for j in range(level):
                    e = jnp.where(j < c, lists[b * n_aux + jnp.minimum(j, c - 1)], total)
                    a = jnp.where(j < c, e // slots, 0)
                    lhs[j * pad : (j + 1) * pad, :] = padded[e]
                    wgt[j * pad : (j + 1) * pad, :] = met_ref[a]
                depth = level * pad
                for i in range(high):
                    res = lax.dot_general(
                        lhs[:depth, i * 128 : (i + 1) * 128],
                        wgt[:depth, :],
                        (((0,), (0,)), ((), ())),
                        preferred_element_type=jnp.float32,
                    ).astype(obuf.dtype)
                    obuf[which, i] = res[:BLK]
                    obuf[which, i + high] = res[BLK:]
                out_copy(obuf.at[which], b, sems.at[which]).start()

            low = level
        return jnp.where(c > 0, used + 1, used)

    used = lax.fori_loop(0, nu_blk, block, 0)
    for w in range(nbuf):

        @pl.when(used > w)
        def _():
            out_copy(obuf.at[w], 0, sems.at[w]).wait()

    def drain(b, _):
        @pl.when(count[b] == 0)
        def _():
            out_copy(zero, b, zsems.at[b]).wait()

        return 0

    lax.fori_loop(0, nu_blk, drain, 0)


def contract(nu_lists, recv, met, occ_local, nu_local):
    n_aux, rows, lanes = recv.shape
    slots = nu_lists.shape[0] // n_aux
    aux_dev = rows // slots
    pad = met.shape[1]
    aux_total = met.shape[2]
    nu_blk = nu_local // BLK
    levels = [v for v in (1, 2, 4, 8, 16, 32, 64) if v < n_aux] + [n_aux]
    nbuf = 4 if nu_blk >= 4 else nu_blk
    return pl.pallas_call(
        functools.partial(
            contract_kernel, n_aux, slots, aux_dev, pad, occ_local, nu_blk, levels
        ),
        out_shape=jax.ShapeDtypeStruct((occ_local, nu_local, aux_total), jnp.bfloat16),
        in_specs=[
            pl.BlockSpec(memory_space=pltpu.SMEM),
            pl.BlockSpec(memory_space=pl.ANY),
            pl.BlockSpec(memory_space=pltpu.VMEM),
        ],
        out_specs=pl.BlockSpec(memory_space=pl.ANY),
        scratch_shapes=[
            pltpu.VMEM(recv.shape, jnp.bfloat16),
            pltpu.VMEM((n_aux * slots + 1, pad, lanes), jnp.bfloat16),
            pltpu.VMEM((n_aux * pad, lanes), jnp.bfloat16),
            pltpu.VMEM((n_aux * pad, aux_total), jnp.bfloat16),
            pltpu.VMEM((nbuf, occ_local, BLK, aux_total), jnp.bfloat16),
            pltpu.VMEM((occ_local, BLK, aux_total), jnp.bfloat16),
            pltpu.SemaphoreType.DMA((nbuf,)),
            pltpu.SemaphoreType.DMA((nu_blk,)),
            pltpu.SemaphoreType.DMA,
            pltpu.SMEM((nu_blk,), jnp.int32),
            pltpu.SMEM((nu_blk * n_aux,), jnp.int32),
        ],
        compiler_params=pltpu.CompilerParams(vmem_limit_bytes=40 * 1024 * 1024),
        name="contract_metric",
    )(nu_lists, recv, met)


def body(integrals, coefficients, metric, mu_blocks, nu_blocks, counts):
    n_aux = lax.axis_size("aux")
    aux_local, slots, _ = integrals.shape
    nbf = coefficients.shape[0] * lax.axis_size("orb")
    nu_local = nbf // lax.axis_size("orb")
    occ_total = coefficients.shape[1]
    occ_local = occ_total // n_aux
    aux_total = metric.shape[1]
    pad = -(-aux_local // 32) * 32

    nu = nu_blocks[0]
    live = jnp.arange(slots) < counts[0, 0]
    same = (nu[:, None] == nu[None, :]) & live[:, None] & live[None, :]
    first = live & ~jnp.any(jnp.tril(same, -1), axis=1)
    keep = same & first[:, None]
    nu_list = jnp.where(first, nu, -1)

    orb = lax.axis_index("orb")
    share = 2 if lax.axis_size("orb") == 2 else 1
    part = aux_local // share
    tall = -(-(part + 1) // 16) * 16
    own_rows = lax.dynamic_slice_in_dim(metric, orb * part if share == 2 else 0, part, 0)
    tail = nu_list.astype(metric.dtype)[None]
    tail = jnp.pad(tail, ((0, tall - part - 1), (0, aux_total - slots)))
    meta = jnp.concatenate([own_rows, tail], axis=0)

    high = occ_local // 2
    coef = listed_coefficients(coefficients, mu_blocks[0], n_aux, high)
    coef = coef.reshape(1, n_aux * high, 2, slots, BLK)
    coef = jnp.where(keep[:, None, None, :, None], coef, jnp.zeros_like(coef))
    coef = coef.reshape(slots * n_aux * high, 2 * slots * BLK)
    blocks = integrals.reshape(aux_local, slots * BLK, BLK)
    msg = half_messages(coef, blocks, n_aux, slots, high)

    recv, *metas = exchange(msg, meta, n_aux, share)
    nu_lists = metas[0][:, part, :slots].astype(jnp.int32).reshape(-1)
    if share == 2:
        swap = orb == 1
        first_rows = jnp.where(swap, metas[1], metas[0])
        second_rows = jnp.where(swap, metas[0], metas[1])
        wide = jnp.concatenate([first_rows[:, :part], second_rows[:, :part]], axis=1)
    else:
        wide = metas[0][:, :part]
    met = wide.reshape(n_aux * aux_local, aux_total).T
    met = met.reshape(n_aux, aux_local, aux_total)
    met = jnp.pad(met, ((0, 0), (0, pad - aux_local), (0, 0)))
    return contract(nu_lists, recv, met, occ_local, nu_local)


def solution(mesh):
    placed = (
        P("aux", "orb", None),
        P("orb", None),
        P("aux", None),
        P("aux", "orb"),
        P("aux", "orb"),
        P("aux", "orb"),
    )
    return jax.shard_map(
        body, mesh=mesh, in_specs=placed, out_specs=P("aux", "orb", None), check_vma=False
    )
```

```python
import functools

import jax
import jax.numpy as jnp
from jax import lax
from jax.experimental import pallas as pl
from jax.experimental.pallas import tpu as pltpu
from jax.sharding import PartitionSpec as P

BLK = 64
MESH = pl.DeviceIdType.MESH


def mate_kernel(mine_ref, both_ref, send_sem, recv_sem, own_sem):
    aux = lax.axis_index("aux")
    orb = lax.axis_index("orb")
    barrier = pltpu.get_barrier_semaphore()
    pl.semaphore_signal(barrier, inc=1, device_id=(aux, 1 - orb), device_id_type=MESH)
    pl.semaphore_wait(barrier, 1)
    copy = pltpu.make_async_remote_copy(
        src_ref=mine_ref,
        dst_ref=both_ref.at[orb],
        send_sem=send_sem,
        recv_sem=recv_sem,
        device_id=(aux, 1 - orb),
        device_id_type=MESH,
    )
    copy.start()
    own = pltpu.make_async_copy(mine_ref, both_ref.at[orb], own_sem)
    own.start()
    own.wait()
    copy.wait_send()
    pltpu.make_async_remote_copy(
        src_ref=mine_ref,
        dst_ref=both_ref.at[1 - orb],
        send_sem=send_sem,
        recv_sem=recv_sem,
        device_id=(aux, 1 - orb),
        device_id_type=MESH,
    ).wait_recv()


def swap_mates(mine, collective_id, name):
    return pl.pallas_call(
        mate_kernel,
        out_shape=jax.ShapeDtypeStruct((2,) + mine.shape, mine.dtype),
        in_specs=[pl.BlockSpec(memory_space=pltpu.VMEM)],
        out_specs=pl.BlockSpec(memory_space=pltpu.VMEM),
        scratch_shapes=[pltpu.SemaphoreType.DMA] * 3,
        compiler_params=pltpu.CompilerParams(
            collective_id=collective_id, has_side_effects=True
        ),
        name=name,
    )(mine)


def arrange(rows, n_aux, high):
    slots = rows.shape[0]
    rows = rows.reshape(slots, BLK, n_aux, 2, high).transpose(2, 4, 3, 0, 1)
    return rows.reshape(n_aux * high, 2 * slots * BLK)


def listed_coefficients(coefficients, mu, n_aux, high):
    slots = mu.shape[0]

    def pick(source, at):
        return jnp.stack(
            [lax.dynamic_slice_in_dim(source, at[s] * BLK, BLK, 0) for s in range(slots)]
        )

    if lax.axis_size("orb") != 2:
        wide = lax.all_gather(coefficients, "orb", axis=0, tiled=True)
        return arrange(pick(wide, mu), n_aux, high)
    orb = lax.axis_index("orb")
    held = coefficients.shape[0] // BLK
    asked = jnp.pad(mu[None], ((0, 7), (0, 128 - slots)))
    asked = swap_mates(asked, 1, "swap_lists")[:, 0, :slots]
    mates = jnp.where(orb == 0, asked[1], asked[0])

    def from_own(at):
        near = at - orb * held
        return arrange(pick(coefficients, jnp.clip(near, 0, held - 1)), n_aux, high)

    given = swap_mates(from_own(mates), 2, "swap_rows")
    given = jnp.where(orb == 0, given[1], given[0])
    mine = from_own(mu)
    near = mu // held == orb
    shape = (n_aux * high, 2, slots, BLK)
    merged = jnp.where(
        near[None, None, :, None], mine.reshape(shape), given.reshape(shape)
    )
    return merged.reshape(mine.shape)


def half_kernel(aux_dev, slots, n_aux, high, coef_ref, blocks_ref, msg_ref, rows_ref):
    def one(p, _):
        x = blocks_ref[p]
        z = jnp.zeros_like(x)
        wide = jnp.concatenate(
            [jnp.concatenate([x, z], axis=1), jnp.concatenate([z, x], axis=1)], axis=0
        )
        part = jnp.dot(coef_ref[...], wide, preferred_element_type=jnp.float32)
        rows_ref[pl.ds(p, part.shape[0], stride=aux_dev), :] = part
        return 0

    lax.fori_loop(0, aux_dev, one, 0, unroll=4)

    def pack(d, _):
        for i in range(high):
            parts = []
            for s in range(slots):
                at = ((s * n_aux + d) * high + i) * aux_dev
                parts.append(rows_ref[pl.ds(pl.multiple_of(at, 8), aux_dev), :])
            msg_ref[d, :, i * 128 : (i + 1) * 128] = jnp.concatenate(parts, axis=0).astype(
                msg_ref.dtype
            )
        return 0

    lax.fori_loop(0, n_aux, pack, 0)


def half_messages(coef, blocks, n_aux, slots, high):
    aux_dev = blocks.shape[0]
    return pl.pallas_call(
        functools.partial(half_kernel, aux_dev, slots, n_aux, high),
        out_shape=jax.ShapeDtypeStruct((n_aux, slots * aux_dev, high * 128), jnp.bfloat16),
        in_specs=[pl.BlockSpec(memory_space=pltpu.VMEM)] * 2,
        out_specs=pl.BlockSpec(memory_space=pltpu.VMEM),
        scratch_shapes=[pltpu.VMEM((coef.shape[0] * aux_dev, 128), jnp.float32)],
        compiler_params=pltpu.CompilerParams(vmem_limit_bytes=40 * 1024 * 1024),
        name="half_messages",
    )(coef, blocks)


def exchange_kernel(
    n, share, msg_ref, meta_ref, recv_ref, *rest
):
    metas_ref, mates_ref = rest[0], (rest[1] if share == 2 else None)
    send_sem, recv_sem, msend_sem, mrecv_sem, own_sem = rest[share:]
    me = lax.axis_index("aux")
    orb = lax.axis_index("orb")
    barrier = pltpu.get_barrier_semaphore()
    for k in range(1, n):
        pl.semaphore_signal(
            barrier, inc=1, device_id=(lax.rem(me + k, n), orb), device_id_type=MESH
        )
    if share == 2:
        pl.semaphore_signal(barrier, inc=1, device_id=(me, 1 - orb), device_id_type=MESH)
    pl.semaphore_wait(barrier, n - 1 + (share == 2))
    by_distance = sorted(range(1, n), key=lambda k: abs(k - n // 2))
    order = []
    while by_distance:
        order.append(by_distance.pop(0))
        if by_distance:
            order.append(by_distance.pop())

    def meta_copy(k, peer, slab):
        return pltpu.make_async_remote_copy(
            src_ref=meta_ref,
            dst_ref=metas_ref.at[slab],
            send_sem=msend_sem.at[k],
            recv_sem=mrecv_sem.at[k],
            device_id=(peer, orb),
            device_id_type=MESH,
        )

    def msg_copy(k, peer, slab):
        return pltpu.make_async_remote_copy(
            src_ref=msg_ref.at[peer],
            dst_ref=recv_ref.at[slab],
            send_sem=send_sem.at[k],
            recv_sem=recv_sem.at[k],
            device_id=(peer, orb),
            device_id_type=MESH,
        )

    for k in order:
        meta_copy(k, lax.rem(me + k, n), me).start()
    for k in order:
        msg_copy(k, lax.rem(me + k, n), me).start()
    own = pltpu.make_async_copy(msg_ref.at[me], recv_ref.at[me], own_sem.at[0])
    own.start()
    own_meta = pltpu.make_async_copy(meta_ref, metas_ref.at[me], own_sem.at[1])
    own_meta.start()
    own_meta.wait()
    for k in order:
        source = lax.rem(me - k + n, n)
        meta_copy(k, source, source).wait_recv()
    if share == 2:
        hand = pltpu.make_async_remote_copy(
            src_ref=metas_ref,
            dst_ref=mates_ref,
            send_sem=msend_sem.at[0],
            recv_sem=mrecv_sem.at[0],
            device_id=(me, 1 - orb),
            device_id_type=MESH,
        )
        hand.start()
        hand.wait()
    own.wait()
    for k in order:
        peer = lax.rem(me + k, n)
        source = lax.rem(me - k + n, n)
        meta_copy(k, peer, me).wait_send()
        msg_copy(k, peer, me).wait_send()
        msg_copy(k, source, source).wait_recv()


def exchange(msg, meta, n, share):
    metas = jax.ShapeDtypeStruct((n,) + meta.shape, meta.dtype)
    return pl.pallas_call(
        functools.partial(exchange_kernel, n, share),
        out_shape=[jax.ShapeDtypeStruct(msg.shape, msg.dtype)] + [metas] * share,
        in_specs=[pl.BlockSpec(memory_space=pl.ANY)] * 2,
        out_specs=[pl.BlockSpec(memory_space=pl.ANY)] * (1 + share),
        scratch_shapes=[pltpu.SemaphoreType.DMA((n,))] * 4 + [pltpu.SemaphoreType.DMA((2,))],
        compiler_params=pltpu.CompilerParams(collective_id=0, has_side_effects=True),
        name="exchange_slots",
    )(msg, meta)


def contract_kernel(
    n_aux, slots, aux_dev, pad, occ_local, nu_blk, levels,
    nu_ref, recv_ref, met_ref, out_ref,
    held, padded, lhs, wgt, obuf, zero, sems, zsems, lsem, count, lists,
):
    total = n_aux * slots
    lanes = occ_local * BLK
    aux_total = out_ref.shape[2]

    load = pltpu.make_async_copy(recv_ref, held, lsem)
    load.start()

    def clear(b, _):
        count[b] = 0
        return 0

    lax.fori_loop(0, nu_blk, clear, 0)

    def enlist(e, _):
        b = nu_ref[e]

        @pl.when(b >= 0)
        def _():
            c = count[b]
            lists[b * n_aux + c] = e
            count[b] = c + 1

        return 0

    lax.fori_loop(0, total, enlist, 0)

    def out_copy(src, b, sem):
        return pltpu.make_async_copy(
            src, out_ref.at[:, pl.ds(pl.multiple_of(b * BLK, BLK), BLK), :], sem
        )

    zero[...] = jnp.zeros_like(zero)

    def empty(b, _):
        @pl.when(count[b] == 0)
        def _():
            out_copy(zero, b, zsems.at[b]).start()

        return 0

    lax.fori_loop(0, nu_blk, empty, 0)
    padded[total] = jnp.zeros((pad, lanes), padded.dtype)
    load.wait()

    def spread(a, _):
        rows = held[a]
        for s in range(slots):
            part = rows[s * aux_dev : (s + 1) * aux_dev]
            padded[a * slots + s] = jnp.concatenate(
                [part, jnp.zeros((pad - aux_dev, lanes), part.dtype)], axis=0
            )
        return 0

    lax.fori_loop(0, n_aux, spread, 0, unroll=2)
    nbuf = obuf.shape[0]
    high = occ_local // 2

    def block(b, used):
        c = count[b]
        which = lax.rem(used, nbuf)

        @pl.when((c > 0) & (used >= nbuf))
        def _():
            out_copy(obuf.at[which], b, sems.at[which]).wait()

        low = 0
        for level in levels:

            @pl.when((c > low) & (c <= level))
            def _(level=level):
                for j in range(level):
                    e = jnp.where(j < c, lists[b * n_aux + jnp.minimum(j, c - 1)], total)
                    a = jnp.where(j < c, e // slots, 0)
                    lhs[j * pad : (j + 1) * pad, :] = padded[e]
                    wgt[j * pad : (j + 1) * pad, :] = met_ref[a]
                depth = level * pad
                for i in range(high):
                    res = lax.dot_general(
                        lhs[:depth, i * 128 : (i + 1) * 128],
                        wgt[:depth, :],
                        (((0,), (0,)), ((), ())),
                        preferred_element_type=jnp.float32,
                    ).astype(obuf.dtype)
                    obuf[which, i] = res[:BLK]
                    obuf[which, i + high] = res[BLK:]
                out_copy(obuf.at[which], b, sems.at[which]).start()

            low = level
        return jnp.where(c > 0, used + 1, used)

    used = lax.fori_loop(0, nu_blk, block, 0)
    for w in range(nbuf):

        @pl.when(used > w)
        def _():
            out_copy(obuf.at[w], 0, sems.at[w]).wait()

    def drain(b, _):
        @pl.when(count[b] == 0)
        def _():
            out_copy(zero, b, zsems.at[b]).wait()

        return 0

    lax.fori_loop(0, nu_blk, drain, 0)


def contract(nu_lists, recv, met, occ_local, nu_local):
    n_aux, rows, lanes = recv.shape
    slots = nu_lists.shape[0] // n_aux
    aux_dev = rows // slots
    pad = met.shape[1]
    aux_total = met.shape[2]
    nu_blk = nu_local // BLK
    levels = [v for v in (1, 2, 4, 8, 16, 32, 64) if v < n_aux] + [n_aux]
    nbuf = 4 if nu_blk >= 4 else nu_blk
    return pl.pallas_call(
        functools.partial(
            contract_kernel, n_aux, slots, aux_dev, pad, occ_local, nu_blk, levels
        ),
        out_shape=jax.ShapeDtypeStruct((occ_local, nu_local, aux_total), jnp.bfloat16),
        in_specs=[
            pl.BlockSpec(memory_space=pltpu.SMEM),
            pl.BlockSpec(memory_space=pl.ANY),
            pl.BlockSpec(memory_space=pltpu.VMEM),
        ],
        out_specs=pl.BlockSpec(memory_space=pl.ANY),
        scratch_shapes=[
            pltpu.VMEM(recv.shape, jnp.bfloat16),
            pltpu.VMEM((n_aux * slots + 1, pad, lanes), jnp.bfloat16),
            pltpu.VMEM((n_aux * pad, lanes), jnp.bfloat16),
            pltpu.VMEM((n_aux * pad, aux_total), jnp.bfloat16),
            pltpu.VMEM((nbuf, occ_local, BLK, aux_total), jnp.bfloat16),
            pltpu.VMEM((occ_local, BLK, aux_total), jnp.bfloat16),
            pltpu.SemaphoreType.DMA((nbuf,)),
            pltpu.SemaphoreType.DMA((nu_blk,)),
            pltpu.SemaphoreType.DMA,
            pltpu.SMEM((nu_blk,), jnp.int32),
            pltpu.SMEM((nu_blk * n_aux,), jnp.int32),
        ],
        compiler_params=pltpu.CompilerParams(vmem_limit_bytes=40 * 1024 * 1024),
        name="contract_metric",
    )(nu_lists, recv, met)


def body(integrals, coefficients, metric, mu_blocks, nu_blocks, counts):
    n_aux = lax.axis_size("aux")
    aux_local, slots, _ = integrals.shape
    nbf = coefficients.shape[0] * lax.axis_size("orb")
    nu_local = nbf // lax.axis_size("orb")
    occ_total = coefficients.shape[1]
    occ_local = occ_total // n_aux
    aux_total = metric.shape[1]
    pad = -(-aux_local // 32) * 32

    nu = nu_blocks[0]
    live = jnp.arange(slots) < counts[0, 0]
    same = (nu[:, None] == nu[None, :]) & live[:, None] & live[None, :]
    first = live & ~jnp.any(jnp.tril(same, -1), axis=1)
    keep = same & first[:, None]
    nu_list = jnp.where(first, nu, -1)

    orb = lax.axis_index("orb")
    share = 2 if lax.axis_size("orb") == 2 else 1
    part = aux_local // share
    tall = -(-(part + 1) // 16) * 16
    own_rows = lax.dynamic_slice_in_dim(metric, orb * part if share == 2 else 0, part, 0)
    tail = nu_list.astype(metric.dtype)[None]
    tail = jnp.pad(tail, ((0, tall - part - 1), (0, aux_total - slots)))
    meta = jnp.concatenate([own_rows, tail], axis=0)

    high = occ_local // 2
    coef = listed_coefficients(coefficients, mu_blocks[0], n_aux, high)
    coef = coef.reshape(1, n_aux * high, 2, slots, BLK)
    coef = jnp.where(keep[:, None, None, :, None], coef, jnp.zeros_like(coef))
    coef = coef.reshape(slots * n_aux * high, 2 * slots * BLK)
    blocks = integrals.reshape(aux_local, slots * BLK, BLK)
    msg = half_messages(coef, blocks, n_aux, slots, high)

    recv, *metas = exchange(msg, meta, n_aux, share)
    nu_lists = metas[0][:, part, :slots].astype(jnp.int32).reshape(-1)
    if share == 2:
        swap = orb == 1
        first_rows = jnp.where(swap, metas[1], metas[0])
        second_rows = jnp.where(swap, metas[0], metas[1])
        wide = jnp.concatenate([first_rows[:, :part], second_rows[:, :part]], axis=1)
    else:
        wide = metas[0][:, :part]
    met = wide.reshape(n_aux * aux_local, aux_total).T
    met = met.reshape(n_aux, aux_local, aux_total)
    met = jnp.pad(met, ((0, 0), (0, pad - aux_local), (0, 0)))
    return contract(nu_lists, recv, met, occ_local, nu_local)


def solution(mesh):
    placed = (
        P("aux", "orb", None),
        P("orb", None),
        P("aux", None),
        P("aux", "orb"),
        P("aux", "orb"),
        P("aux", "orb"),
    )
    return jax.shard_map(
        body, mesh=mesh, in_specs=placed, out_specs=P("aux", "orb", None), check_vma=False
    )
```
